256 devices in a mesh: dp: 8 (over y, core), seq: 32 (over x, z).
Axes of the slice: x: 4, y: 4, z: 8, core: 2. Of those that a mesh axis runs over, the one named last changes fastest.
Arguments:
- waveform: bfloat16 [8, 1024, 1360], P('dp', 'seq'), may hold values from -6 to 6
- packing: int32 [8, 1024], P(None, 'seq'), may hold values from 0 to 255, as said below
- live_frames: int32 [8, 1024], P('dp', 'seq'), may hold values from 1 to 4
- placing: int32 [8, 1024], P('dp'), may hold values from 0 to 1023, as said below
- first_kernel: bfloat16 [10, 512], replicated, may hold values from -2 to 2
- middle_kernels: bfloat16 [4, 1536, 512], replicated, may hold values from -0.15625 to 0.15625
- last_kernels: bfloat16 [2, 1024, 512], replicated, may hold values from -0.1875 to 0.1875
- norm_gain: float32 [512], replicated, may hold values from 0.1 to 1.9
- norm_bias: float32 [512], replicated, may hold values from -3 to 3
- projection: bfloat16 [512, 1920], replicated, may hold values from -0.25 to 0.25
- projection_bias: float32 [1920], replicated, may hold values from -3 to 3
Outputs:
- encoded: bfloat16 [8, 4096, 1920], P('dp', 'seq')
The draws below stay inside these ranges and needn't reach their ends.
Inputs may be any that keep to these rules, and one draw needn't show every extreme that they name: For every seq block s, the entries packing[d, s * 32 + k] over all d and k < 32 hold each number below 256 once, and each row d takes exactly 4 of them from each row r (the numbers r * 32 to (r + 1) * 32 - 1). `placing`: each row holds each number below 1024 once; each aligned block of 32 positions takes exactly one number from each aligned block of 32 numbers.
All inputs are finite; a program needn't handle non-finite values.
Results may differ from the reference program's by a relative error of at most 0.02.
Values may be sent and summed in bfloat16 or wider, within the bound.
A program may use at most 128 MiB of HBM per device.

```python
import jax
import jax.numpy as jnp
from jax import lax

CHANNELS = 512
WIDTH = 1920
CF = 4
CH_DEV = 32
CS = 1360
SPANS_ROW = 1024
BATCH_ROWS = 8


def balanced_table(key, groups, per_group):
    portion = per_group // groups
    key_rows, key_inner, key_order = jax.random.split(key, 3)
    row_ids = jnp.arange(groups, dtype=jnp.int32)[:, None]
    slot_ids = jnp.arange(per_group, dtype=jnp.int32)[None, :]
    base = (row_ids + slot_ids) % groups
    sources = jax.random.permutation(key_rows, groups).astype(jnp.int32)[base]
    ranking = row_ids * portion + slot_ids // groups
    inner = jax.vmap(lambda single: jax.random.permutation(single, per_group))(jax.random.split(key_inner, groups)).astype(jnp.int32)
    values = sources * per_group + inner[sources, ranking]
    orders = jax.vmap(lambda single: jax.random.permutation(single, per_group))(jax.random.split(key_order, groups)).astype(jnp.int32)
    return jnp.take_along_axis(values, orders, axis=1)


def draw_packing(key, part):
    key = jax.random.fold_in(key, 11)
    column_count = SPANS_ROW // CH_DEV
    keys = jax.random.split(key, column_count)
    tables = jax.vmap(lambda single: balanced_table(single, BATCH_ROWS, CH_DEV))(keys)
    return tables.transpose(1, 0, 2).reshape(BATCH_ROWS, SPANS_ROW).astype(jnp.int32)


def draw_live_frames(key, part):
    key = jax.random.fold_in(key, 23)
    key_counts, key_full = jax.random.split(key)
    frame_counts = jax.random.randint(key_counts, (BATCH_ROWS, SPANS_ROW), 1, 2 * CF)
    frame_counts = jnp.minimum(frame_counts, CF)
    full_column = jax.random.randint(key_full, (BATCH_ROWS, 1), 0, SPANS_ROW)
    columns = jnp.arange(SPANS_ROW, dtype=jnp.int32)[None, :]
    frame_counts = jnp.where(columns == full_column, CF, frame_counts)
    return frame_counts.astype(jnp.int32)


def draw_placing(key, part):
    key = jax.random.fold_in(key, 37)
    keys = jax.random.split(key, BATCH_ROWS)
    tables = jax.vmap(lambda single: balanced_table(single, SPANS_ROW // CH_DEV, CH_DEV))(keys)
    return tables.reshape(BATCH_ROWS, SPANS_ROW).astype(jnp.int32)


def shard_levels(rng, shape, shards, low, top_value):
    loudness, own = 1.0, jax.random.fold_in(rng, 6)
    for dim, parts in shards:
        steps = jnp.exp(jax.random.uniform(jax.random.fold_in(own, dim), (parts,), jnp.float32, low / len(shards), top_value / len(shards)))
        loudness = loudness * jnp.repeat(steps, shape[dim] // parts).reshape([-1 if axis == dim else 1 for axis in range(len(shape))])
    return loudness


def scatter_about(key, shape, width, reach, shards=(), held_as=jnp.bfloat16):
    result = jax.random.normal(key, shape, jnp.float32) * width
    if len(shards) > 0:
        result = shard_levels(key, shape, shards, -0.22, 0.18) * result
    return jnp.clip(result, min=-reach, max=reach).astype(held_as)


def setup_inputs(seed: int = 0) -> dict:
    seeds = jax.random.split(jax.random.key(seed), 12)
    return {
        "waveform": scatter_about(seeds[0], (BATCH_ROWS, SPANS_ROW, CS), 1.0, 6.0, ((0, 8), (1, 32))),
        "packing": draw_packing(jax.random.fold_in(seeds[11], 71), 0),
        "live_frames": draw_live_frames(jax.random.fold_in(seeds[11], 71), 0),
        "placing": draw_placing(jax.random.fold_in(seeds[11], 71), 0),
        "first_kernel": scatter_about(seeds[4], (10, CHANNELS), 10 ** -0.5, 2.0),
        "middle_kernels": scatter_about(seeds[5], (4, 3 * CHANNELS, CHANNELS), (3 * CHANNELS) ** -0.5, 0.15625),
        "last_kernels": scatter_about(seeds[6], (2, 2 * CHANNELS, CHANNELS), (2 * CHANNELS) ** -0.5, 0.1875),
        "norm_gain": jnp.clip(1.0 + 0.18 * jax.random.normal(seeds[7], (CHANNELS,), jnp.float32), 0.1, 1.9),
        "norm_bias": scatter_about(seeds[8], (CHANNELS,), 0.5, 3.0, (), jnp.float32),
        "projection": scatter_about(seeds[9], (CHANNELS, WIDTH), CHANNELS ** -0.5, 0.25),
        "projection_bias": scatter_about(seeds[10], (WIDTH,), 0.5, 3.0, (), jnp.float32),
    }


def settle(hidden):
    average = lax.optimization_barrier(jnp.mean(hidden, axis=-1, keepdims=True))
    centered = hidden - average
    spread = lax.optimization_barrier(jnp.mean(centered * centered, axis=-1, keepdims=True))
    return centered * lax.rsqrt(spread + 1e-05)

def activate(hidden):
    return jax.nn.gelu(settle(hidden), approximate=False).astype(jnp.bfloat16)

def kernel_three(signal, kernel):
    length, channels = signal.shape
    steps_out = (length - 1) // 2
    padded = jnp.concatenate([signal, jnp.zeros((1, channels), signal.dtype)], axis=0)
    padded = padded.reshape((length + 1) // 2, 2 * channels)
    head = jnp.dot(padded[:steps_out], kernel[:2 * channels], preferred_element_type=jnp.float32)
    tail = jnp.dot(padded[1:steps_out + 1, :channels], kernel[2 * channels:], preferred_element_type=jnp.float32)
    return head + tail

def kernel_two(signal, kernel):
    length, channels = signal.shape
    paired = signal.reshape(length // 2, 2 * channels)
    return jnp.dot(paired, kernel, preferred_element_type=jnp.float32)

def extract(span_wave, first_kernel, middle_kernels, last_kernels, norm_gain, norm_bias):
    sample_rows = span_wave.reshape(-1, 5)
    window = jnp.concatenate([sample_rows[:-1], sample_rows[1:]], axis=1)
    signal = activate(jnp.dot(window, first_kernel, preferred_element_type=jnp.float32))
    for layer_index in range(4):
        signal = activate(kernel_three(signal, middle_kernels[layer_index]))
    for layer_index in range(2):
        signal = activate(kernel_two(signal, last_kernels[layer_index]))
    return (settle(signal.astype(jnp.float32)) * norm_gain + norm_bias).astype(jnp.bfloat16)

def reference(waveform, packing, live_frames, placing, first_kernel, middle_kernels, last_kernels, norm_gain, norm_bias, projection, projection_bias):
    rows_dp, spans_row, samples = waveform.shape
    columns = jnp.arange(spans_row, dtype=jnp.int32)[None, :]
    source = packing // CH_DEV * spans_row + columns // CH_DEV * CH_DEV + packing % CH_DEV
    source = source.reshape(-1).astype(jnp.int32)
    routed = jnp.take(waveform.reshape(-1, samples), source, axis=0)
    routed_live = jnp.take(live_frames.reshape(-1), source)
    frame_index = jnp.arange(CF, dtype=jnp.int32)

    def one_span(span_item):
        span_wave, span_live = span_item
        ready = extract(span_wave, first_kernel, middle_kernels, last_kernels, norm_gain, norm_bias)
        projected = jnp.dot(ready, projection, preferred_element_type=jnp.float32) + projection_bias
        return jnp.where((frame_index < span_live)[:, None], projected, jnp.zeros_like(projected)).astype(jnp.bfloat16)
    features = lax.map(one_span, (routed, routed_live))
    features = features.reshape(rows_dp, spans_row, CF, features.shape[-1])
    placed = jax.vmap(lambda table, index: jnp.take(table, index, axis=0))(features, placing)
    return placed.reshape(rows_dp, spans_row * CF, features.shape[-1])
```

```python
import jax, jax.numpy as jnp
from jax import lax
from jax.experimental import pallas as pl
from jax.experimental.pallas import tpu as pltpu
BF=jnp.bfloat16; F32=jnp.float32
C=512
NB=32
RG=32

def gelu(z):
    half=z*0.5
    return half*lax.erf(z*0.7071067811865476)+half
def act_rows(h):
    v=jnp.mean(h*h,axis=1,keepdims=True)
    return gelu(h*lax.rsqrt(v+1e-5)).astype(BF)
def center(w):
    w=w.astype(F32)
    return w-jnp.mean(w,axis=1,keepdims=True)

PLAN={0:(271,16),1:(135,15),2:(67,17),3:(33,11),4:(16,8),5:(8,8),6:(4,4)}
def nchunk(l): return -(-PLAN[l][0]//PLAN[l][1])
MAXM=max(v[1] for v in PLAN.values())*NB

def pipeline(n,mm,el,hA,hB):
    mm(0,hA)
    if n==1:
        el(0,hA); return
    def body(j,_):
        mm(2*j+1,hB); el(2*j,hA)
        mm(2*j+2,hA); el(2*j+1,hB)
        return 0
    full=(n-1)//2
    if full>1: lax.fori_loop(0,full,body,0)
    elif full==1: body(0,0)
    if n%2==0:
        mm(n-1,hB); el(n-2,hA); el(n-1,hB)
    else:
        el(n-1,hA)

def build_lhs(xf,lhs):
    for t in range(272):
        o=5*t; j=o//128*128; o-=j
        if o<=118:
            v=xf[:,j:j+128]
            v=pltpu.roll(v,(128-o)%128,1) if o else v
        else:
            v=pltpu.roll(xf[:,j:j+256],256-o,1)[:,:128]
        lhs[t*NB:(t+1)*NB,:]=v.astype(BF)

def extract(xf,w0,wm,wl,lhs,acts,hA,hB):
    build_lhs(xf,lhs)
    for l in range(7):
        T,Tc=PLAN[l]; M=Tc*NB; n=nchunk(l)
        out=acts[l]
        def mm(i,h,l=l,M=M,Tc=Tc):
            if l==0:
                a=lhs[pl.ds(pl.multiple_of(i*M,M),M),:]
                a=jnp.concatenate([a,a],axis=1); w=w0[...]
            else:
                src=acts[l-1]
                s3=src.reshape(src.shape[0]//64,64,C)
                t0=i*Tc
                a=[s3[pl.ds(t0,Tc),0:32,:].reshape(M,C),s3[pl.ds(t0,Tc),32:64,:].reshape(M,C)]
                if l<=4:
                    a.append(s3[pl.ds(t0+1,Tc),0:32,:].reshape(M,C)); w=wm[l-1]
                else: w=wl[l-5]
                a=jnp.concatenate(a,axis=1)
            h[0:M,:]=jnp.dot(a,w,preferred_element_type=F32)
        def el(i,h,l=l,M=M,out=out):
            for r in range(0,M,RG):
                out[pl.ds(pl.multiple_of(i*M,M)+r,RG),:]=act_rows(h[r:r+RG,:])
        pipeline(n,mm,el,hA,hB)

def act_scratch():
    out=[]
    for l in range(7):
        need=nchunk(l)*PLAN[l][1]
        if l<6:
            nxt=nchunk(l+1)*PLAN[l+1][1]
            need=max(need,2*nxt+(2 if l+1<=4 else 0))
        need+=need%2
        out.append(pltpu.VMEM((need*NB,C),BF))
    return out
from jax.sharding import PartitionSpec as P


def kern(x,w0,wm_h,wl_h,gain,bias,o,xf,w0s,wm,wl,lhs,*rest):
    acts=rest[:7]; hA,hB,sem=rest[7:]
    cps=[pltpu.make_async_copy(wm_h,wm,sem.at[0]),pltpu.make_async_copy(wl_h,wl,sem.at[1])]
    for c in cps: c.start()
    xf[:,1280:1536]=jnp.zeros((32,256),F32)
    xf[:,0:1360]=x[...].astype(F32)
    wc=center(w0[...]); hi=wc.astype(BF)
    w0s[...]=jnp.zeros((256,C),BF)
    w0s[0:10,:]=hi; w0s[128:138,:]=(wc-hi.astype(F32)).astype(BF)
    for c in cps: c.wait()
    for l in range(4):
        def b(i,_):
            r=pl.ds(pl.multiple_of(i*128,128),128)
            wm[l,r,:]=center(wm[l,r,:]).astype(BF); return 0
        lax.fori_loop(0,12,b,0)
    for l in range(2):
        def b(i,_):
            r=pl.ds(pl.multiple_of(i*128,128),128)
            wl[l,r,:]=center(wl[l,r,:]).astype(BF); return 0
        lax.fori_loop(0,8,b,0)
    extract(xf,w0s,wm,wl,lhs,acts,hA,hB)
    a=acts[6][0:128,:].astype(F32)
    d=a-jnp.mean(a,axis=1,keepdims=True)
    v=jnp.mean(d*d,axis=1,keepdims=True)
    o[...]=(d*lax.rsqrt(v+1e-5)*gain[...]+bias[...]).astype(BF)
V=pl.BlockSpec(memory_space=pltpu.VMEM); A=pl.BlockSpec(memory_space=pl.ANY)
def call(x,w0,wm,wl,g,b):
    return pl.pallas_call(kern,out_shape=jax.ShapeDtypeStruct((128,C),BF),in_specs=[V,V,A,A,V,V],out_specs=V,
     scratch_shapes=[pltpu.VMEM((32,1536),F32),pltpu.VMEM((256,C),BF),pltpu.VMEM((4,1536,C),BF),pltpu.VMEM((2,1024,C),BF),pltpu.VMEM((272*32,128),BF)]+act_scratch()+[pltpu.VMEM((MAXM,C),F32)]*2+[pltpu.SemaphoreType.DMA((2,))],
     compiler_params=pltpu.CompilerParams(vmem_limit_bytes=60*2**20),name="compute")(x,w0,wm,wl,g,b)


def outgoing(table, owner, per_group):
    groups = table.shape[0]
    portion = per_group // groups
    owned = (table // per_group == owner).astype(jnp.int32)
    ranking = jnp.cumsum(owned, axis=1) - 1
    targets = jnp.arange(portion, dtype=jnp.int32)[None, :, None]
    selected = (owned[:, None, :] == 1) & (ranking[:, None, :] == targets)
    locals_index = jnp.where(selected, (table % per_group)[:, None, :], 0)
    return jnp.sum(locals_index, axis=2).reshape(-1)


def incoming(own_row, per_group, groups):
    portion = per_group // groups
    sources = own_row // per_group
    places = jnp.arange(per_group, dtype=jnp.int32)
    earlier = (sources[:, None] == sources[None, :]) & (places[None, :] <= places[:, None])
    ranking = jnp.sum(earlier.astype(jnp.int32), axis=1) - 1
    return sources * portion + ranking


DEAD = 2.0**100


def body(
    waveform,
    packing,
    live_frames,
    placing,
    first_kernel,
    middle_kernels,
    last_kernels,
    norm_gain,
    norm_bias,
    projection,
    projection_bias,
):
    per_device = waveform.shape[1]
    samples = waveform.shape[2]
    row_count = lax.axis_size("dp")
    shard_count = lax.axis_size("seq")
    dp_index = lax.axis_index("dp")
    seq_index = lax.axis_index("seq")
    own_packing = lax.dynamic_index_in_dim(packing, dp_index, 0, keepdims=False)
    outward = outgoing(packing, dp_index, per_device)
    portion = per_device // row_count
    whole = jnp.concatenate([waveform[0], live_frames[0][:, None].astype(BF)], axis=1)
    send_wave = jnp.take(whole, outward, axis=0).reshape(row_count, portion, samples + 1)
    came_wave = lax.all_to_all(send_wave, "dp", split_axis=0, concat_axis=0, tiled=True)
    inward = incoming(own_packing, per_device, row_count)
    placing_row = placing[0]
    place_table = placing_row.reshape(shard_count, per_device)
    own_places = lax.dynamic_slice_in_dim(placing_row, seq_index * per_device, per_device)
    outward_frames = outgoing(place_table, seq_index, per_device)
    order = jnp.take(inward, outward_frames)
    chosen = jnp.take(came_wave.reshape(-1, samples + 1), order, axis=0)
    ready = call(
        chosen[:, :samples],
        first_kernel,
        middle_kernels,
        last_kernels,
        norm_gain.reshape(1, C),
        norm_bias.reshape(1, C),
    ).reshape(4, NB, C)
    alive = jnp.arange(4)[:, None] < chosen[:, samples].astype(jnp.int32)[None, :]
    ready = jnp.where(alive[:, :, None], ready, jnp.asarray(DEAD, BF))
    came = lax.all_to_all(ready.transpose(1, 0, 2), "seq", split_axis=0, concat_axis=0, tiled=True)
    arrived = jnp.take(came, own_places // per_device, axis=0).reshape(per_device * 4, C)
    projected = (
        jnp.dot(arrived, projection, preferred_element_type=F32) + projection_bias
    )
    dead = arrived[:, :1] > DEAD / 2
    return jnp.where(dead, 0.0, projected).astype(BF)[None]


def solution(mesh):
    placed = (
        P("dp", "seq", None),
        P(None, "seq"),
        P("dp", "seq"),
        P("dp", None),
        P(),
        P(),
        P(),
        P(),
        P(),
        P(),
        P(),
    )
    return jax.shard_map(
        body, mesh=mesh, in_specs=placed, out_specs=P("dp", "seq", None), check_vma=False
    )
```

```python
import jax, jax.numpy as jnp
from jax import lax
from jax.experimental import pallas as pl
from jax.experimental.pallas import tpu as pltpu
BF=jnp.bfloat16; F32=jnp.float32
C=512
NB=32
RG=32

def gelu(z):
    half=z*0.5
    return half*lax.erf(z*0.7071067811865476)+half
def act_rows(h):
    v=jnp.mean(h*h,axis=1,keepdims=True)
    return gelu(h*lax.rsqrt(v+1e-5)).astype(BF)
def center(w):
    w=w.astype(F32)
    return w-jnp.mean(w,axis=1,keepdims=True)

PLAN={0:(271,16),1:(135,15),2:(67,17),3:(33,11),4:(16,8),5:(8,8),6:(4,4)}
def nchunk(l): return -(-PLAN[l][0]//PLAN[l][1])
MAXM=max(v[1] for v in PLAN.values())*NB

def pipeline(n,mm,el,hA,hB):
    mm(0,hA)
    if n==1:
        el(0,hA); return
    def body(j,_):
        mm(2*j+1,hB); el(2*j,hA)
        mm(2*j+2,hA); el(2*j+1,hB)
        return 0
    full=(n-1)//2
    if full>1: lax.fori_loop(0,full,body,0)
    elif full==1: body(0,0)
    if n%2==0:
        mm(n-1,hB); el(n-2,hA); el(n-1,hB)
    else:
        el(n-1,hA)

def build_lhs(xf,lhs):
    for t in range(272):
        o=5*t; j=o//128*128; o-=j
        if o<=118:
            v=xf[:,j:j+128]
            v=pltpu.roll(v,(128-o)%128,1) if o else v
        else:
            v=pltpu.roll(xf[:,j:j+256],256-o,1)[:,:128]
        lhs[t*NB:(t+1)*NB,:]=v.astype(BF)

def extract(xf,w0,wm,wl,lhs,acts,hA,hB):
    build_lhs(xf,lhs)
    for l in range(7):
        T,Tc=PLAN[l]; M=Tc*NB; n=nchunk(l)
        out=acts[l]
        def mm(i,h,l=l,M=M,Tc=Tc):
            if l==0:
                a=lhs[pl.ds(pl.multiple_of(i*M,M),M),:]
                a=jnp.concatenate([a,a],axis=1); w=w0[...]
            else:
                src=acts[l-1]
                s3=src.reshape(src.shape[0]//64,64,C)
                t0=i*Tc
                a=[s3[pl.ds(t0,Tc),0:32,:].reshape(M,C),s3[pl.ds(t0,Tc),32:64,:].reshape(M,C)]
                if l<=4:
                    a.append(s3[pl.ds(t0+1,Tc),0:32,:].reshape(M,C)); w=wm[l-1]
                else: w=wl[l-5]
                a=jnp.concatenate(a,axis=1)
            h[0:M,:]=jnp.dot(a,w,preferred_element_type=F32)
        def el(i,h,l=l,M=M,out=out):
            base=pl.multiple_of(i*M,M)
            def rows(r,_):
                out[pl.ds(base+r*RG,RG),:]=act_rows(h[pl.ds(r*RG,RG),:])
                return 0
            lax.fori_loop(0,M//RG,rows,0,unroll=True)
        pipeline(n,mm,el,hA,hB)

def act_scratch():
    out=[]
    for l in range(7):
        need=nchunk(l)*PLAN[l][1]
        if l<6:
            nxt=nchunk(l+1)*PLAN[l+1][1]
            need=max(need,2*nxt+(2 if l+1<=4 else 0))
        need+=need%2
        out.append(pltpu.VMEM((need*NB,C),BF))
    return out
from jax.sharding import PartitionSpec as P


MESH=pl.DeviceIdType.MESH
I32=jnp.int32
ROWS=8
SHARDS=32
TILES=11
SLAB=48
SAMPLES=1360
DEAD=2.0**100

def iota(shape,dim): return lax.broadcasted_iota(I32,shape,dim)
def earlier_counts(owned):
    tri=(iota((NB,NB),0)<iota((NB,NB),1)).astype(F32).astype(BF)
    return jnp.dot(owned.astype(F32).astype(BF),tri,preferred_element_type=F32)

def dp_peer(k):
    return lax.rem(lax.axis_index("dp")+k,ROWS)
def seq_peer(k):
    return lax.rem(lax.axis_index("seq")+k,SHARDS)
def row_of_shard(s):
    return lax.rem(s,4)*8+s//4

def greet():
    barrier=pltpu.get_barrier_semaphore()
    def a(k,_):
        pl.semaphore_signal(barrier,inc=1,device_id={"dp":dp_peer(k)},device_id_type=MESH); return 0
    lax.fori_loop(1,ROWS,a,0)
    def b(k,_):
        pl.semaphore_signal(barrier,inc=1,device_id={"seq":seq_peer(k)},device_id_type=MESH); return 0
    lax.fori_loop(1,SHARDS,b,0)
    return barrier

def pack_waves(wave,packing,live,xa,tall,send):
    me=lax.axis_index("dp")
    xa[:,1280:1408]=jnp.zeros((NB,128),BF)
    xa[:,0:SAMPLES]=wave[...]
    table=packing[...]
    owned=(table>>5)==me
    count=earlier_counts(owned)
    parts=[]
    for i in range(4):
        chosen=owned&(count==float(i))
        index=jnp.sum(jnp.where(chosen,table&31,0),axis=1,keepdims=True)
        parts.append(jnp.where(iota((8,NB),1)==index,1.0,0.0))
    pick=jnp.concatenate(parts,axis=0)
    lives=jnp.sum(pick*live[...].astype(F32),axis=1,keepdims=True)
    pick=pick.astype(BF)
    y=jnp.dot(pick,xa[...],preferred_element_type=F32)
    for j in range(TILES):
        tile=y[:,j*128:(j+1)*128]
        if j==TILES-1:
            tile=jnp.where(iota((NB,128),1)==SAMPLES-1280,lives,tile)
        for i in range(4):
            tall[pl.ds(i*TILES+j,8,stride=SLAB),:]=tile[i*8:(i+1)*8,:]
    for d in range(ROWS):
        send[d]=tall[d*SLAB:(d+1)*SLAB,:].astype(BF)

def wave_copy(k,send,recv,ssem,rsem):
    return pltpu.make_async_remote_copy(src_ref=send.at[dp_peer(k)],dst_ref=recv.at[lax.axis_index("dp")],
        send_sem=ssem.at[k],recv_sem=rsem.at[k],device_id={"dp":dp_peer(k)},device_id_type=MESH)
def frame_copy(k,send,recv,ssem,rsem):
    return pltpu.make_async_remote_copy(src_ref=send.at[row_of_shard(seq_peer(k))],dst_ref=recv.at[lax.axis_index("seq")],
        send_sem=ssem.at[k],recv_sem=rsem.at[k],device_id={"seq":seq_peer(k)},device_id_type=MESH)

def order_rows(packing,placing):
    me_d,me_s=lax.axis_index("dp"),lax.axis_index("seq")
    own=packing[pl.ds(me_d,1),:]
    owned=(own>>5)==iota((ROWS,NB),0)
    count=earlier_counts(owned)
    slots=jnp.concatenate([jnp.where(owned&(count==float(i)),1.0,0.0) for i in range(4)],axis=0)
    table=placing[...]
    parts=[]
    for g in range(4):
        mine=((table>>5)==me_s)&((iota((8,128),1)>>5)==g)
        index=jnp.sum(jnp.where(mine,table&31,0),axis=1,keepdims=True)
        parts.append(jnp.where(iota((8,NB),1)==index,1.0,0.0))
    taken=jnp.concatenate(parts,axis=0)
    return lax.dot_general(taken.astype(BF),slots.astype(BF),(((1,),(1,)),((),())),preferred_element_type=F32).astype(BF)

def unpack_waves(recv,order,tall,xa,xf):
    for r in range(ROWS):
        tall[r*SLAB:(r+1)*SLAB,:]=recv[r].astype(F32)
    for j in range(TILES):
        tile=jnp.concatenate([tall[pl.ds(i*TILES+j,8,stride=SLAB),:] for i in range(4)],axis=0)
        xa[:,j*128:(j+1)*128]=tile.astype(BF)
    xf[:,0:1408]=jnp.dot(order,xa[...],preferred_element_type=F32)
    xf[:,1408:1536]=jnp.zeros((NB,128),F32)

def frame_order(placing):
    me=lax.axis_index("seq")
    row=placing[pl.ds(me//4,1),:]
    at=lax.rem(me,4)*32
    shape=(128,128)
    hit=iota(shape,1)==at+(iota(shape,0)>>2)
    source=jnp.sum(jnp.where(hit,row>>5,0),axis=1,keepdims=True)
    return jnp.where(iota(shape,1)==source*4+(iota(shape,0)&3),1.0,0.0).astype(BF)

def pack_frames(act,lives,gain,bias,tall,send):
    for f in range(4):
        a=act[f*NB:(f+1)*NB,:].astype(F32)
        d=a-jnp.mean(a,axis=1,keepdims=True)
        v=jnp.mean(d*d,axis=1,keepdims=True)
        ready=d*lax.rsqrt(v+1e-5)*gain[...]+bias[...]
        ready=jnp.where(lives>f+0.5,ready,DEAD)
        for j in range(4):
            tall[pl.ds(f*4+j,NB,stride=16),:]=ready[:,j*128:(j+1)*128]
    for b in range(NB):
        send[b]=tall[b*16:(b+1)*16,:].astype(BF)

def unpack_frames(recv,order,tall,out):
    for s in range(SHARDS):
        tall[s*16:(s+1)*16,:]=recv[s].astype(F32)
    a=jnp.concatenate([tall[pl.ds(j,128,stride=4),:] for j in range(4)],axis=1).astype(BF)
    out[...]=jnp.dot(order,a,preferred_element_type=F32).astype(BF)

def center_all(ref,depth):
    for l in range(ref.shape[0]):
        def b(i,_):
            r=pl.ds(pl.multiple_of(i*128,128),128)
            ref[l,r,:]=center(ref[l,r,:]).astype(BF); return 0
        lax.fori_loop(0,depth//128,b,0)

def mega(wave,packing,live,placing,w0,wm_h,wl_h,gain,bias,out,
         xf,w0s,wm,wl,lhs,*rest):
    acts=rest[:7]
    hA,hB,xa,tall,tall2,send1,recv1,send2,recv2,wsem,s1,r1,s2,r2=rest[7:]
    cps=[pltpu.make_async_copy(wm_h.at[l],wm.at[l],wsem.at[l]) for l in range(4)]
    cps+=[pltpu.make_async_copy(wl_h.at[l],wl.at[l],wsem.at[4+l]) for l in range(2)]
    for c in cps: c.start()
    barrier=greet()
    pack_waves(wave,packing,live,xa,tall,send1)
    pl.semaphore_wait(barrier,ROWS-1+SHARDS-1)
    def go(k,_):
        wave_copy(k,send1,recv1,s1,r1).start(); return 0
    lax.fori_loop(1,ROWS,go,0)
    me=lax.axis_index("dp")
    recv1[me]=send1[me]
    order=order_rows(packing,placing)
    forder=frame_order(placing)
    wc=center(w0[...]); hi=wc.astype(BF)
    w0s[...]=jnp.zeros((256,C),BF)
    w0s[0:10,:]=hi; w0s[128:138,:]=(wc-hi.astype(F32)).astype(BF)
    for c in cps: c.wait()
    center_all(wm,1536); center_all(wl,1024)
    def done(k,_):
        wave_copy(k,send1,recv1,s1,r1).wait(); return 0
    lax.fori_loop(1,ROWS,done,0)
    unpack_waves(recv1,order,tall,xa,xf)
    extract(xf,w0s,wm,wl,lhs,acts,hA,hB)
    lives=jnp.sum(jnp.where(iota((NB,128),1)==SAMPLES-1280,xf[:,1280:1408],0.0),axis=1,keepdims=True)
    pack_frames(acts[6],lives,gain,bias,tall2,send2)
    def go2(k,_):
        frame_copy(k,send2,recv2,s2,r2).start(); return 0
    lax.fori_loop(1,SHARDS,go2,0)
    ms=lax.axis_index("seq")
    recv2[ms]=send2[row_of_shard(ms)]
    def done2(k,_):
        frame_copy(k,send2,recv2,s2,r2).wait(); return 0
    lax.fori_loop(1,SHARDS,done2,0)
    unpack_frames(recv2,forder,tall2,out)

def call_mega(wave,packing,live,placing,w0,wm,wl,g,b):
    V=pl.BlockSpec(memory_space=pltpu.VMEM); A=pl.BlockSpec(memory_space=pl.ANY)
    D=pltpu.SemaphoreType.DMA
    return pl.pallas_call(mega,out_shape=jax.ShapeDtypeStruct((128,C),BF),
     in_specs=[V,V,V,V,V,A,A,V,V],out_specs=V,
     scratch_shapes=[pltpu.VMEM((32,1536),F32),pltpu.VMEM((256,C),BF),pltpu.VMEM((4,1536,C),BF),pltpu.VMEM((2,1024,C),BF),
       pltpu.VMEM((272*32,128),BF)]+act_scratch()+[pltpu.VMEM((MAXM,C),F32)]*2+[
       pltpu.VMEM((NB,1408),BF),pltpu.VMEM((ROWS*SLAB,128),F32),pltpu.VMEM((SHARDS*16,128),F32),
       pltpu.VMEM((ROWS,SLAB,128),BF),pltpu.VMEM((ROWS,SLAB,128),BF),pltpu.VMEM((SHARDS,16,128),BF),pltpu.VMEM((SHARDS,16,128),BF),
       D((6,)),D((ROWS,)),D((ROWS,)),D((SHARDS,)),D((SHARDS,))],
     compiler_params=pltpu.CompilerParams(vmem_limit_bytes=60*2**20,collective_id=0,has_side_effects=True),name="extract")(
       wave,packing,live,placing,w0,wm,wl,g,b)


def body(
    waveform,
    packing,
    live_frames,
    placing,
    first_kernel,
    middle_kernels,
    last_kernels,
    norm_gain,
    norm_bias,
    projection,
    projection_bias,
):
    arrived = call_mega(
        waveform[0],
        packing,
        live_frames,
        placing.reshape(8, 128),
        first_kernel,
        middle_kernels,
        last_kernels,
        norm_gain.reshape(1, C),
        norm_bias.reshape(1, C),
    )
    projected = (
        jnp.dot(arrived, projection, preferred_element_type=F32) + projection_bias
    )
    dead = arrived[:, :1] > DEAD / 2
    return jnp.where(dead, 0.0, projected).astype(BF)[None]


def solution(mesh):
    placed = (
        P("dp", "seq", None),
        P(None, "seq"),
        P("dp", "seq"),
        P("dp", None),
        P(),
        P(),
        P(),
        P(),
        P(),
        P(),
        P(),
    )
    return jax.shard_map(
        body, mesh=mesh, in_specs=placed, out_specs=P("dp", "seq", None), check_vma=False
    )
```

```python
import jax, jax.numpy as jnp
from jax import lax
from jax.experimental import pallas as pl
from jax.experimental.pallas import tpu as pltpu
BF=jnp.bfloat16; F32=jnp.float32
C=512
NB=32
RG=32

def act_rows(h,eps):
    total=jnp.sum(h*h,axis=1,keepdims=True)
    y=h*lax.rsqrt(total*(2.0/C)+2.0*eps)
    return (y*lax.erf(y)+y).astype(BF)
def center(w):
    w=w.astype(F32)
    return w-jnp.mean(w,axis=1,keepdims=True)

F1=8
EPS=1e-05
PLAN={0:(272,16),1:(136,8),2:(67,17),3:(33,11),4:(16,8),5:(8,8),6:(4,4)}
def nchunk(l): return -(-PLAN[l][0]//PLAN[l][1])
HM=max(max(v[1] for v in PLAN.values())*NB,2*F1*NB)
GM=F1*NB

def pipeline(n,mm,el,hA,hB):
    mm(0,hA)
    if n==1:
        el(0,hA); return
    def body(j,_):
        mm(2*j+1,hB); el(2*j,hA)
        mm(2*j+2,hA); el(2*j+1,hB)
        return 0
    full=(n-1)//2
    if full>1: lax.fori_loop(0,full,body,0)
    elif full==1: body(0,0)
    if n%2==0:
        mm(n-1,hB); el(n-2,hA); el(n-1,hB)
    else:
        el(n-1,hA)

def build_lhs(xf,lhs):
    for t in range(272):
        o=5*t; j=o//128*128; o-=j
        if o<=118:
            v=xf[:,j:j+128]
            v=pltpu.roll(v,(128-o)%128,1) if o else v
        else:
            v=pltpu.roll(xf[:,j:j+256],256-o,1)[:,:128]
        lhs[t*NB:(t+1)*NB,:]=v.astype(BF)

def first_two(lhs,w0,w1,pair,act1,hs,gs):
    n=136//F1; M1=F1*NB; M0=2*M1; E=2*NB
    def mm0(i,h):
        a=lhs[pl.ds(pl.multiple_of(i*M0,M0),M0),:]
        h[0:M0,:]=jnp.dot(jnp.concatenate([a,a],axis=1),w0[...],preferred_element_type=F32)
    def mm1(g,src):
        v=src.reshape(F1+1,2*NB,C)
        a=jnp.concatenate([v[0:F1,0:NB,:].reshape(M1,C),v[0:F1,NB:2*NB,:].reshape(M1,C),
            v[1:F1+1,0:NB,:].reshape(M1,C)],axis=1)
        g[0:M1,:]=jnp.dot(a,w1[...],preferred_element_type=F32)
    def el0(h,out,nxt):
        for r in range(0,M0,RG):
            v=act_rows(h[r:r+RG,:],EPS)
            out[E+r:E+r+RG,:]=v
            if r>=M0-E: nxt[r-(M0-E):r-(M0-E)+RG,:]=v
    def el1(i,g):
        base=pl.multiple_of(i*M1,M1)
        for r in range(0,M1,RG):
            act1[pl.ds(base+r,RG),:]=act_rows(g[r:r+RG,:],2*EPS)
    def step(i,par,m0=True,e0=True,m1=True,e1=True):
        if m0: mm0(i+1,hs[1-par])
        if m1: mm1(gs[1-par],pair[1-par])
        if e0: el0(hs[par],pair[par],pair[1-par])
        if e1: el1(i-2,gs[par])
    mm0(0,hs[0])
    step(0,0,m1=False,e1=False)
    step(1,1,e1=False)
    pairs=(n-3)//2
    def body(j,_):
        step(2+2*j,0); step(3+2*j,1)
        return 0
    lax.fori_loop(0,pairs,body,0)
    for i in range(2+2*pairs,n+2):
        step(i,i%2,m0=i+1<n,e0=i<n,m1=0<=i-1<n,e1=0<=i-2<n)

def extract(xf,w0,wm,wl,lhs,acts,hA,hB,gA,gB):
    build_lhs(xf,lhs)
    first_two(lhs,w0,wm.at[0],acts[0:2],acts[2],(hA,hB),(gA,gB))
    for l in range(2,7):
        T,Tc=PLAN[l]; M=Tc*NB; n=nchunk(l)
        out=acts[l+1]
        def mm(i,h,l=l,M=M,Tc=Tc):
            src=acts[l]
            s3=src.reshape(src.shape[0]//64,64,C)
            t0=i*Tc
            if l==2:
                a=[s3[pl.ds(t0,Tc),32:64,:],s3[pl.ds(t0+1,Tc),0:32,:],s3[pl.ds(t0+1,Tc),32:64,:]]
            else:
                a=[s3[pl.ds(t0,Tc),0:32,:],s3[pl.ds(t0,Tc),32:64,:]]
                if l<=4: a.append(s3[pl.ds(t0+1,Tc),0:32,:])
            a=[v.reshape(M,C) for v in a]
            w=wm[l-1] if l<=4 else wl[l-5]
            h[0:M,:]=jnp.dot(jnp.concatenate(a,axis=1),w,preferred_element_type=F32)
        def el(i,h,l=l,M=M,out=out):
            base=pl.multiple_of(i*M,M)
            def rows(r,_):
                out[pl.ds(base+r*RG,RG),:]=act_rows(h[pl.ds(r*RG,RG),:],2*EPS)
                return 0
            lax.fori_loop(0,M//RG,rows,0,unroll=True)
        pipeline(n,mm,el,hA,hB)

def act_scratch():
    frames=[2*F1+2,2*F1+2,138,68,34,16,8,4]
    return [pltpu.VMEM((f*NB,C),BF) for f in frames]
from jax.sharding import PartitionSpec as P


MESH=pl.DeviceIdType.MESH
I32=jnp.int32
ROWS=8
SHARDS=32
TILES=11
SLAB=48
SAMPLES=1360
WIDTH=1920
DEAD=2.0**100

def iota(shape,dim): return lax.broadcasted_iota(I32,shape,dim)
def earlier_counts(owned):
    tri=(iota((NB,NB),0)<iota((NB,NB),1)).astype(F32).astype(BF)
    return jnp.dot(owned.astype(F32).astype(BF),tri,preferred_element_type=F32)

def dp_peer(k):
    return lax.rem(lax.axis_index("dp")+k,ROWS)
def seq_peer(k):
    return lax.rem(lax.axis_index("seq")+k,SHARDS)
def row_of_shard(s):
    return lax.rem(s,4)*8+s//4

def greet():
    barrier=pltpu.get_barrier_semaphore()
    def a(k,_):
        pl.semaphore_signal(barrier,inc=1,device_id={"dp":dp_peer(k)},device_id_type=MESH); return 0
    lax.fori_loop(1,ROWS,a,0)
    def b(k,_):
        pl.semaphore_signal(barrier,inc=1,device_id={"seq":seq_peer(k)},device_id_type=MESH); return 0
    lax.fori_loop(1,SHARDS,b,0)
    return barrier

def pack_waves(wave,packing,live,xa,tall,send):
    me=lax.axis_index("dp")
    xa[:,1280:1408]=jnp.zeros((NB,128),BF)
    xa[:,0:SAMPLES]=wave[...]
    table=packing[...]
    owned=(table>>5)==me
    count=earlier_counts(owned)
    parts=[]
    for i in range(4):
        chosen=owned&(count==float(i))
        index=jnp.sum(jnp.where(chosen,table&31,0),axis=1,keepdims=True)
        parts.append(jnp.where(iota((8,NB),1)==index,1.0,0.0))
    pick=jnp.concatenate(parts,axis=0)
    lives=jnp.sum(pick*live[...].astype(F32),axis=1,keepdims=True)
    pick=pick.astype(BF)
    y=jnp.dot(pick,xa[...],preferred_element_type=F32)
    for j in range(TILES):
        tile=y[:,j*128:(j+1)*128]
        if j==TILES-1:
            tile=jnp.where(iota((NB,128),1)==SAMPLES-1280,lives,tile)
        for i in range(4):
            tall[pl.ds(i*TILES+j,8,stride=SLAB),:]=tile[i*8:(i+1)*8,:]
    for d in range(ROWS):
        send[d]=tall[d*SLAB:(d+1)*SLAB,:].astype(BF)

def wave_copy(k,send,recv,ssem,rsem):
    return pltpu.make_async_remote_copy(src_ref=send.at[dp_peer(k)],dst_ref=recv.at[lax.axis_index("dp")],
        send_sem=ssem.at[k],recv_sem=rsem.at[k],device_id={"dp":dp_peer(k)},device_id_type=MESH)
def frame_copy(k,send,recv,ssem,rsem):
    return pltpu.make_async_remote_copy(src_ref=send.at[row_of_shard(seq_peer(k))],dst_ref=recv.at[lax.axis_index("seq")],
        send_sem=ssem.at[k],recv_sem=rsem.at[k],device_id={"seq":seq_peer(k)},device_id_type=MESH)

def order_rows(packing,placing):
    me_d,me_s=lax.axis_index("dp"),lax.axis_index("seq")
    own=packing[pl.ds(me_d,1),:]
    owned=(own>>5)==iota((ROWS,NB),0)
    count=earlier_counts(owned)
    slots=jnp.concatenate([jnp.where(owned&(count==float(i)),1.0,0.0) for i in range(4)],axis=0)
    table=placing[...]
    parts=[]
    for g in range(4):
        mine=((table>>5)==me_s)&((iota((8,128),1)>>5)==g)
        index=jnp.sum(jnp.where(mine,table&31,0),axis=1,keepdims=True)
        parts.append(jnp.where(iota((8,NB),1)==index,1.0,0.0))
    taken=jnp.concatenate(parts,axis=0)
    return lax.dot_general(taken.astype(BF),slots.astype(BF),(((1,),(1,)),((),())),preferred_element_type=F32).astype(BF)

def unpack_waves(recv,order,tall,xa,xf):
    for r in range(ROWS):
        tall[r*SLAB:(r+1)*SLAB,:]=recv[r].astype(F32)
    for j in range(TILES):
        tile=jnp.concatenate([tall[pl.ds(i*TILES+j,8,stride=SLAB),:] for i in range(4)],axis=0)
        xa[:,j*128:(j+1)*128]=tile.astype(BF)
    xf[:,0:1408]=jnp.dot(order,xa[...],preferred_element_type=F32)
    xf[:,1408:1536]=jnp.zeros((NB,128),F32)

def frame_order(placing):
    me=lax.axis_index("seq")
    row=placing[pl.ds(me//4,1),:]
    at=lax.rem(me,4)*32
    shape=(128,128)
    hit=iota(shape,1)==at+(iota(shape,0)>>2)
    source=jnp.sum(jnp.where(hit,row>>5,0),axis=1,keepdims=True)
    return jnp.where(iota(shape,1)==source*4+(iota(shape,0)&3),1.0,0.0).astype(BF)

def pack_frames(act,lives,gain,bias,tall,send):
    for f in range(4):
        a=act[f*NB:(f+1)*NB,:].astype(F32)
        d=a-jnp.mean(a,axis=1,keepdims=True)
        v=jnp.mean(d*d,axis=1,keepdims=True)
        ready=d*lax.rsqrt(v+2*EPS)*gain[...]+bias[...]
        ready=jnp.where(lives>f+0.5,ready,DEAD)
        for j in range(4):
            tall[pl.ds(f*4+j,NB,stride=16),:]=ready[:,j*128:(j+1)*128]
    for b in range(NB):
        send[b]=tall[b*16:(b+1)*16,:].astype(BF)

def unpack_frames(recv,order,tall,proj,proj_bias,out):
    for s in range(SHARDS):
        tall[s*16:(s+1)*16,:]=recv[s].astype(F32)
    a=jnp.concatenate([tall[pl.ds(j,128,stride=4),:] for j in range(4)],axis=1).astype(BF)
    ready=jnp.dot(order,a,preferred_element_type=F32)
    dead=ready[:,0:1]>DEAD/2
    ready=ready.astype(BF)
    for j in range(0,WIDTH,384):
        p=jnp.dot(ready,proj[:,j:j+384],preferred_element_type=F32)+proj_bias[:,j:j+384]
        out[:,j:j+384]=jnp.where(dead,0.0,p).astype(BF)

def center_all(ref,depth):
    for l in range(ref.shape[0]):
        def b(i,_):
            r=pl.ds(pl.multiple_of(i*512,512),512)
            ref[l,r,:]=center(ref[l,r,:]).astype(BF); return 0
        lax.fori_loop(0,depth//512,b,0)

def mega(wave,packing,live,placing,w0,wm_h,wl_h,gain,bias,proj_h,proj_bias,out,
         xf,w0s,wm,wl,lhs,*rest):
    acts=rest[:8]
    hA,hB,gA,gB,proj,xa,tall,tall2,send1,recv1,send2,recv2,wsem,s1,r1,s2,r2=rest[8:]
    cps=[pltpu.make_async_copy(wm_h.at[l],wm.at[l],wsem.at[l]) for l in range(4)]
    cps+=[pltpu.make_async_copy(wl_h.at[l],wl.at[l],wsem.at[4+l]) for l in range(2)]
    cps+=[pltpu.make_async_copy(proj_h,proj,wsem.at[6])]
    for c in cps: c.start()
    barrier=greet()
    pack_waves(wave,packing,live,xa,tall,send1)
    pl.semaphore_wait(barrier,ROWS-1+SHARDS-1)
    def go(k,_):
        wave_copy(k,send1,recv1,s1,r1).start(); return 0
    lax.fori_loop(1,ROWS,go,0)
    me=lax.axis_index("dp")
    recv1[me]=send1[me]
    order=order_rows(packing,placing)
    forder=frame_order(placing)
    wc=center(w0[...]); hi=wc.astype(BF)
    w0s[...]=jnp.zeros((256,C),BF)
    w0s[0:10,:]=hi; w0s[128:138,:]=(wc-hi.astype(F32)).astype(BF)
    for c in cps: c.wait()
    center_all(wm,1536); center_all(wl,1024)
    def done(k,_):
        wave_copy(k,send1,recv1,s1,r1).wait(); return 0
    lax.fori_loop(1,ROWS,done,0)
    unpack_waves(recv1,order,tall,xa,xf)
    extract(xf,w0s,wm,wl,lhs,acts,hA,hB,gA,gB)
    lives=jnp.sum(jnp.where(iota((NB,128),1)==SAMPLES-1280,xf[:,1280:1408],0.0),axis=1,keepdims=True)
    pack_frames(acts[7],lives,gain,bias,tall2,send2)
    def go2(k,_):
        frame_copy(k,send2,recv2,s2,r2).start(); return 0
    lax.fori_loop(1,SHARDS,go2,0)
    ms=lax.axis_index("seq")
    recv2[ms]=send2[row_of_shard(ms)]
    def done2(k,_):
        frame_copy(k,send2,recv2,s2,r2).wait(); return 0
    lax.fori_loop(1,SHARDS,done2,0)
    unpack_frames(recv2,forder,tall2,proj,proj_bias,out)

def call_mega(wave,packing,live,placing,w0,wm,wl,g,b,proj,proj_bias):
    V=pl.BlockSpec(memory_space=pltpu.VMEM); A=pl.BlockSpec(memory_space=pl.ANY)
    D=pltpu.SemaphoreType.DMA
    return pl.pallas_call(mega,out_shape=jax.ShapeDtypeStruct((128,WIDTH),BF),
     in_specs=[V,V,V,V,V,A,A,V,V,A,V],out_specs=V,
     scratch_shapes=[pltpu.VMEM((32,1536),F32),pltpu.VMEM((256,C),BF),pltpu.VMEM((4,1536,C),BF),pltpu.VMEM((2,1024,C),BF),
       pltpu.VMEM((272*32,128),BF)]+act_scratch()+[pltpu.VMEM((HM,C),F32)]*2+[pltpu.VMEM((GM,C),F32)]*2+[pltpu.VMEM((C,WIDTH),BF),
       pltpu.VMEM((NB,1408),BF),pltpu.VMEM((ROWS*SLAB,128),F32),pltpu.VMEM((SHARDS*16,128),F32),
       pltpu.VMEM((ROWS,SLAB,128),BF),pltpu.VMEM((ROWS,SLAB,128),BF),pltpu.VMEM((SHARDS,16,128),BF),pltpu.VMEM((SHARDS,16,128),BF),
       D((7,)),D((ROWS,)),D((ROWS,)),D((SHARDS,)),D((SHARDS,))],
     compiler_params=pltpu.CompilerParams(vmem_limit_bytes=60*2**20,collective_id=0,has_side_effects=True),name="extract")(
       wave,packing,live,placing,w0,wm,wl,g,b,proj,proj_bias)


def body(
    waveform,
    packing,
    live_frames,
    placing,
    first_kernel,
    middle_kernels,
    last_kernels,
    norm_gain,
    norm_bias,
    projection,
    projection_bias,
):
    encoded = call_mega(
        waveform[0],
        packing,
        live_frames,
        placing.reshape(8, 128),
        first_kernel,
        middle_kernels,
        last_kernels,
        norm_gain.reshape(1, C),
        norm_bias.reshape(1, C),
        projection,
        projection_bias.reshape(1, WIDTH),
    )
    return encoded[None]


def solution(mesh):
    placed = (
        P("dp", "seq", None),
        P(None, "seq"),
        P("dp", "seq"),
        P("dp", None),
        P(),
        P(),
        P(),
        P(),
        P(),
        P(),
        P(),
    )
    return jax.shard_map(
        body, mesh=mesh, in_specs=placed, out_specs=P("dp", "seq", None), check_vma=False
    )
```

```python
import jax, jax.numpy as jnp
from jax import lax
from jax.experimental import pallas as pl
from jax.experimental.pallas import tpu as pltpu
BF=jnp.bfloat16; F32=jnp.float32
C=512
NB=32
RG=32

def act_rows(h,eps):
    total=jnp.sum(h*h,axis=1,keepdims=True)
    y=h*lax.rsqrt(total*(2.0/C)+2.0*eps)
    return (y*lax.erf(y)+y).astype(BF)
def center(w):
    w=w.astype(F32)
    return w-jnp.mean(w,axis=1,keepdims=True)

F1=34
EPS=1e-05
PLAN={0:(272,16),1:(136,8),2:(67,17),3:(33,11),4:(16,8),5:(8,8),6:(4,4)}
def nchunk(l): return -(-PLAN[l][0]//PLAN[l][1])
HM=max(max(v[1] for v in PLAN.values())*NB,2*F1*NB)
GM=F1*NB

def pipeline(n,mm,el,hA,hB):
    mm(0,hA)
    if n==1:
        el(0,hA); return
    def body(j,_):
        mm(2*j+1,hB); el(2*j,hA)
        mm(2*j+2,hA); el(2*j+1,hB)
        return 0
    full=(n-1)//2
    if full>1: lax.fori_loop(0,full,body,0)
    elif full==1: body(0,0)
    if n%2==0:
        mm(n-1,hB); el(n-2,hA); el(n-1,hB)
    else:
        el(n-1,hA)

def build_lhs(xf,lhs,first,last):
    for t in range(first,last):
        o=5*t; j=o//128*128; o-=j
        if o<=118:
            v=xf[:,j:j+128]
            v=pltpu.roll(v,(128-o)%128,1) if o else v
        else:
            v=pltpu.roll(xf[:,j:j+256],256-o,1)[:,:128]
        lhs[t*NB:(t+1)*NB,:]=v.astype(BF)

def first_two(xf,lhs,w0,w1,pair,act1,hs,gs):
    n=136//F1; M1=F1*NB; M0=2*M1; E=2*NB
    def mm0(i,h):
        a=lhs[i*M0:(i+1)*M0,:]
        h[0:M0,:]=jnp.dot(jnp.concatenate([a,a],axis=1),w0[...],preferred_element_type=F32)
    def mm1(g,src):
        v=src.reshape(F1+1,2*NB,C)
        a=jnp.concatenate([v[0:F1,0:NB,:].reshape(M1,C),v[0:F1,NB:2*NB,:].reshape(M1,C),
            v[1:F1+1,0:NB,:].reshape(M1,C)],axis=1)
        g[0:M1,:]=jnp.dot(a,w1[...],preferred_element_type=F32)
    def el0(h,out,nxt):
        for r in range(0,M0,RG):
            v=act_rows(h[r:r+RG,:],EPS)
            out[E+r:E+r+RG,:]=v
            if r>=M0-E: nxt[r-(M0-E):r-(M0-E)+RG,:]=v
    def el1(i,g):
        for r in range(i*M1,(i+1)*M1,RG):
            act1[r:r+RG,:]=act_rows(g[r-i*M1:r-i*M1+RG,:],2*EPS)
    def step(i,par,m0=True,e0=True,m1=True,e1=True):
        if i+2<n: build_lhs(xf,lhs,(i+2)*2*F1,(i+3)*2*F1)
        if m0: mm0(i+1,hs[1-par])
        if m1: mm1(gs[1-par],pair[1-par])
        if e0: el0(hs[par],pair[par],pair[1-par])
        if e1: el1(i-2,gs[par])
    def edge(i):
        step(i,i%2,m0=i+1<n,e0=i<n,m1=0<=i-1<n,e1=0<=i-2<n)
    build_lhs(xf,lhs,0,4*F1)
    mm0(0,hs[0])
    for i in range(n+2): edge(i)

def extract(xf,w0,wm,wl,lhs,acts,hA,hB,gA,gB):
    first_two(xf,lhs,w0,wm.at[0],acts[0:2],acts[2],(hA,hB),(gA,gB))
    for l in range(2,7):
        T,Tc=PLAN[l]; M=Tc*NB; n=nchunk(l)
        out=acts[l+1]
        def mm(i,h,l=l,M=M,Tc=Tc):
            src=acts[l]
            s3=src.reshape(src.shape[0]//64,64,C)
            t0=i*Tc
            if l==2:
                a=[s3[pl.ds(t0,Tc),32:64,:],s3[pl.ds(t0+1,Tc),0:32,:],s3[pl.ds(t0+1,Tc),32:64,:]]
            else:
                a=[s3[pl.ds(t0,Tc),0:32,:],s3[pl.ds(t0,Tc),32:64,:]]
                if l<=4: a.append(s3[pl.ds(t0+1,Tc),0:32,:])
            a=[v.reshape(M,C) for v in a]
            w=wm[l-1] if l<=4 else wl[l-5]
            h[0:M,:]=jnp.dot(jnp.concatenate(a,axis=1),w,preferred_element_type=F32)
        def el(i,h,l=l,M=M,out=out):
            base=pl.multiple_of(i*M,M)
            def rows(r,_):
                out[pl.ds(base+r*RG,RG),:]=act_rows(h[pl.ds(r*RG,RG),:],2*EPS)
                return 0
            lax.fori_loop(0,M//RG,rows,0,unroll=True)
        pipeline(n,mm,el,hA,hB)

def act_scratch():
    frames=[2*F1+2,2*F1+2,138,68,34,16,8,4]
    return [pltpu.VMEM((f*NB,C),BF) for f in frames]
from jax.sharding import PartitionSpec as P


MESH=pl.DeviceIdType.MESH
I32=jnp.int32
ROWS=8
SHARDS=32
TILES=11
SLAB=48
SAMPLES=1360
WIDTH=1920
DEAD=2.0**100

def iota(shape,dim): return lax.broadcasted_iota(I32,shape,dim)
def earlier_counts(owned):
    tri=(iota((NB,NB),0)<iota((NB,NB),1)).astype(F32).astype(BF)
    return jnp.dot(owned.astype(F32).astype(BF),tri,preferred_element_type=F32)

def dp_peer(k):
    return lax.rem(lax.axis_index("dp")+k,ROWS)
def seq_peer(k):
    return lax.rem(lax.axis_index("seq")+k,SHARDS)
def row_of_shard(s):
    return lax.rem(s,4)*8+s//4

def greet():
    barrier=pltpu.get_barrier_semaphore()
    def a(k,_):
        pl.semaphore_signal(barrier,inc=1,device_id={"dp":dp_peer(k)},device_id_type=MESH); return 0
    lax.fori_loop(1,ROWS,a,0)
    def b(k,_):
        pl.semaphore_signal(barrier,inc=1,device_id={"seq":seq_peer(k)},device_id_type=MESH); return 0
    lax.fori_loop(1,SHARDS,b,0)
    return barrier

def pack_waves(wave,packing,live,xa,tall,send):
    me=lax.axis_index("dp")
    xa[:,1280:1408]=jnp.zeros((NB,128),BF)
    xa[:,0:SAMPLES]=wave[...]
    table=packing[...]
    owned=(table>>5)==me
    count=earlier_counts(owned)
    parts=[]
    for i in range(4):
        chosen=owned&(count==float(i))
        index=jnp.sum(jnp.where(chosen,table&31,0),axis=1,keepdims=True)
        parts.append(jnp.where(iota((8,NB),1)==index,1.0,0.0))
    pick=jnp.concatenate(parts,axis=0)
    lives=jnp.sum(pick*live[...].astype(F32),axis=1,keepdims=True)
    pick=pick.astype(BF)
    y=jnp.dot(pick,xa[...],preferred_element_type=F32)
    for j in range(TILES):
        tile=y[:,j*128:(j+1)*128]
        if j==TILES-1:
            tile=jnp.where(iota((NB,128),1)==SAMPLES-1280,lives,tile)
        for i in range(4):
            tall[pl.ds(i*TILES+j,8,stride=SLAB),:]=tile[i*8:(i+1)*8,:]
    for d in range(ROWS):
        send[d]=tall[d*SLAB:(d+1)*SLAB,:].astype(BF)

def wave_copy(k,send,recv,ssem,rsem):
    return pltpu.make_async_remote_copy(src_ref=send.at[dp_peer(k)],dst_ref=recv.at[lax.axis_index("dp")],
        send_sem=ssem.at[k],recv_sem=rsem.at[k],device_id={"dp":dp_peer(k)},device_id_type=MESH)
def frame_copy(k,send,recv,ssem,rsem):
    return pltpu.make_async_remote_copy(src_ref=send.at[row_of_shard(seq_peer(k))],dst_ref=recv.at[lax.axis_index("seq")],
        send_sem=ssem.at[k],recv_sem=rsem.at[k],device_id={"seq":seq_peer(k)},device_id_type=MESH)

def order_rows(packing,placing):
    me_d,me_s=lax.axis_index("dp"),lax.axis_index("seq")
    own=packing[pl.ds(me_d,1),:]
    owned=(own>>5)==iota((ROWS,NB),0)
    count=earlier_counts(owned)
    slots=jnp.concatenate([jnp.where(owned&(count==float(i)),1.0,0.0) for i in range(4)],axis=0)
    table=placing[...]
    parts=[]
    for g in range(4):
        mine=((table>>5)==me_s)&((iota((8,128),1)>>5)==g)
        index=jnp.sum(jnp.where(mine,table&31,0),axis=1,keepdims=True)
        parts.append(jnp.where(iota((8,NB),1)==index,1.0,0.0))
    taken=jnp.concatenate(parts,axis=0)
    return lax.dot_general(taken.astype(BF),slots.astype(BF),(((1,),(1,)),((),())),preferred_element_type=F32).astype(BF)

def unpack_waves(recv,order,tall,xa,xf):
    for r in range(ROWS):
        tall[r*SLAB:(r+1)*SLAB,:]=recv[r].astype(F32)
    for j in range(TILES):
        tile=jnp.concatenate([tall[pl.ds(i*TILES+j,8,stride=SLAB),:] for i in range(4)],axis=0)
        xa[:,j*128:(j+1)*128]=tile.astype(BF)
    xf[:,0:1408]=jnp.dot(order,xa[...],preferred_element_type=F32)
    xf[:,1408:1536]=jnp.zeros((NB,128),F32)

def frame_order(placing):
    me=lax.axis_index("seq")
    row=placing[pl.ds(me//4,1),:]
    at=lax.rem(me,4)*32
    shape=(128,128)
    hit=iota(shape,1)==at+(iota(shape,0)>>2)
    source=jnp.sum(jnp.where(hit,row>>5,0),axis=1,keepdims=True)
    return jnp.where(iota(shape,1)==source*4+(iota(shape,0)&3),1.0,0.0).astype(BF)

def pack_frames(act,lives,gain,bias,tall,send):
    for f in range(4):
        a=act[f*NB:(f+1)*NB,:].astype(F32)
        d=a-jnp.mean(a,axis=1,keepdims=True)
        v=jnp.mean(d*d,axis=1,keepdims=True)
        ready=d*lax.rsqrt(v+2*EPS)*gain[...]+bias[...]
        ready=jnp.where(lives>f+0.5,ready,DEAD)
        for j in range(4):
            tall[pl.ds(f*4+j,NB,stride=16),:]=ready[:,j*128:(j+1)*128]
    for b in range(NB):
        send[b]=tall[b*16:(b+1)*16,:].astype(BF)

def unpack_frames(recv,order,tall,proj,proj_bias,out):
    for s in range(SHARDS):
        tall[s*16:(s+1)*16,:]=recv[s].astype(F32)
    a=jnp.concatenate([tall[pl.ds(j,128,stride=4),:] for j in range(4)],axis=1).astype(BF)
    ready=jnp.dot(order,a,preferred_element_type=F32)
    dead=ready[:,0:1]>DEAD/2
    ready=ready.astype(BF)
    for j in range(0,WIDTH,384):
        p=jnp.dot(ready,proj[:,j:j+384],preferred_element_type=F32)+proj_bias[:,j:j+384]
        out[:,j:j+384]=jnp.where(dead,0.0,p).astype(BF)

def center_all(ref,depth,copies):
    for l in range(ref.shape[0]):
        copies[l].wait()
        def b(i,_):
            r=pl.ds(pl.multiple_of(i*512,512),512)
            ref[l,r,:]=center(ref[l,r,:]).astype(BF); return 0
        lax.fori_loop(0,depth//512,b,0)

def mega(wave,packing,live,placing,w0,wm_h,wl_h,gain,bias,proj_h,proj_bias,out,
         xf,w0s,wm,wl,lhs,*rest):
    acts=rest[:8]
    hA,hB,gA,gB,proj,xa,tall,tall2,send1,recv1,send2,recv2,wsem,s1,r1,s2,r2=rest[8:]
    cps=[pltpu.make_async_copy(wm_h.at[l],wm.at[l],wsem.at[l]) for l in range(4)]
    cps+=[pltpu.make_async_copy(wl_h.at[l],wl.at[l],wsem.at[4+l]) for l in range(2)]
    cps+=[pltpu.make_async_copy(proj_h,proj,wsem.at[6])]
    for c in cps: c.start()
    barrier=greet()
    pack_waves(wave,packing,live,xa,tall,send1)
    pl.semaphore_wait(barrier,ROWS-1+SHARDS-1)
    def go(k,_):
        wave_copy(k,send1,recv1,s1,r1).start(); return 0
    lax.fori_loop(1,ROWS,go,0)
    me=lax.axis_index("dp")
    recv1[me]=send1[me]
    order=order_rows(packing,placing)
    forder=frame_order(placing)
    wc=center(w0[...]); hi=wc.astype(BF)
    w0s[...]=jnp.zeros((256,C),BF)
    w0s[0:10,:]=hi; w0s[128:138,:]=(wc-hi.astype(F32)).astype(BF)
    center_all(wm,1536,cps[0:4]); center_all(wl,1024,cps[4:6])
    def done(k,_):
        wave_copy(k,send1,recv1,s1,r1).wait(); return 0
    lax.fori_loop(1,ROWS,done,0)
    unpack_waves(recv1,order,tall,xa,xf)
    extract(xf,w0s,wm,wl,lhs,acts,hA,hB,gA,gB)
    lives=jnp.sum(jnp.where(iota((NB,128),1)==SAMPLES-1280,xf[:,1280:1408],0.0),axis=1,keepdims=True)
    pack_frames(acts[7],lives,gain,bias,tall2,send2)
    def go2(k,_):
        frame_copy(k,send2,recv2,s2,r2).start(); return 0
    lax.fori_loop(1,SHARDS,go2,0)
    ms=lax.axis_index("seq")
    recv2[ms]=send2[row_of_shard(ms)]
    def done2(k,_):
        frame_copy(k,send2,recv2,s2,r2).wait(); return 0
    lax.fori_loop(1,SHARDS,done2,0)
    cps[6].wait()
    unpack_frames(recv2,forder,tall2,proj,proj_bias,out)

def call_mega(wave,packing,live,placing,w0,wm,wl,g,b,proj,proj_bias):
    V=pl.BlockSpec(memory_space=pltpu.VMEM); A=pl.BlockSpec(memory_space=pl.ANY)
    D=pltpu.SemaphoreType.DMA
    return pl.pallas_call(mega,out_shape=pltpu.VMEM((128,WIDTH),BF),
     in_specs=[V,V,V,V,V,A,A,V,V,A,V],out_specs=V,
     scratch_shapes=[pltpu.VMEM((32,1536),F32),pltpu.VMEM((256,C),BF),pltpu.VMEM((4,1536,C),BF),pltpu.VMEM((2,1024,C),BF),
       pltpu.VMEM((272*32,128),BF)]+act_scratch()+[pltpu.VMEM((HM,C),F32)]*2+[pltpu.VMEM((GM,C),F32)]*2+[pltpu.VMEM((C,WIDTH),BF),
       pltpu.VMEM((NB,1408),BF),pltpu.VMEM((ROWS*SLAB,128),F32),pltpu.VMEM((SHARDS*16,128),F32),
       pltpu.VMEM((ROWS,SLAB,128),BF),pltpu.VMEM((ROWS,SLAB,128),BF),pltpu.VMEM((SHARDS,16,128),BF),pltpu.VMEM((SHARDS,16,128),BF),
       D((7,)),D((ROWS,)),D((ROWS,)),D((SHARDS,)),D((SHARDS,))],
     compiler_params=pltpu.CompilerParams(vmem_limit_bytes=60*2**20,collective_id=0,has_side_effects=True),name="extract")(
       wave,packing,live,placing,w0,wm,wl,g,b,proj,proj_bias)


def body(
    waveform,
    packing,
    live_frames,
    placing,
    first_kernel,
    middle_kernels,
    last_kernels,
    norm_gain,
    norm_bias,
    projection,
    projection_bias,
):
    encoded = call_mega(
        waveform[0],
        packing,
        live_frames,
        placing.reshape(8, 128),
        first_kernel,
        middle_kernels,
        last_kernels,
        norm_gain.reshape(1, C),
        norm_bias.reshape(1, C),
        projection,
        projection_bias.reshape(1, WIDTH),
    )
    return encoded[None]


def solution(mesh):
    placed = (
        P("dp", "seq", None),
        P(None, "seq"),
        P("dp", "seq"),
        P("dp", None),
        P(),
        P(),
        P(),
        P(),
        P(),
        P(),
        P(),
    )
    return jax.shard_map(
        body, mesh=mesh, in_specs=placed, out_specs=P("dp", "seq", None), check_vma=False
    )
```

```python
import jax, jax.numpy as jnp
from jax import lax
from jax.experimental import pallas as pl
from jax.experimental.pallas import tpu as pltpu
BF=jnp.bfloat16; F32=jnp.float32
C=512
NB=32
RG=32

def act_rows(h,eps):
    total=jnp.sum(h*h,axis=1,keepdims=True)
    y=h*lax.rsqrt(total*(2.0/C)+2.0*eps)
    return (y*lax.erf(y)+y).astype(BF)
def center(w):
    w=w.astype(F32)
    return w-jnp.mean(w,axis=1,keepdims=True)

F1=34
EPS=1e-05
PLAN={0:(272,16),1:(136,8),2:(67,17),3:(33,11),4:(16,8),5:(8,8),6:(4,4)}
def nchunk(l): return -(-PLAN[l][0]//PLAN[l][1])
HM=max(max(v[1] for v in PLAN.values())*NB,2*F1*NB)
GM=F1*NB

def pipeline(n,mm,el,hA,hB):
    mm(0,hA)
    if n==1:
        el(0,hA); return
    def body(j,_):
        mm(2*j+1,hB); el(2*j,hA)
        mm(2*j+2,hA); el(2*j+1,hB)
        return 0
    full=(n-1)//2
    if full>1: lax.fori_loop(0,full,body,0)
    elif full==1: body(0,0)
    if n%2==0:
        mm(n-1,hB); el(n-2,hA); el(n-1,hB)
    else:
        el(n-1,hA)

def build_lhs(xf,lhs,first,last):
    for t in range(first,last):
        o=5*t; j=o//128*128; o-=j
        if o<=118:
            v=xf[:,j:j+128]
            v=pltpu.roll(v,(128-o)%128,1) if o else v
        else:
            v=pltpu.roll(xf[:,j:j+256],256-o,1)[:,:128]
        lhs[t*NB:(t+1)*NB,:]=v.astype(BF)

def first_two(xf,lhs,w0,w1,pair,act1,hs,gs):
    n=136//F1; M1=F1*NB; M0=2*M1; E=2*NB
    def mm0(i,h):
        a=lhs[i*M0:(i+1)*M0,:]
        h[0:M0,:]=jnp.dot(jnp.concatenate([a,a],axis=1),w0[...],preferred_element_type=F32)
    def mm1(g,src):
        v=src.reshape(F1+1,2*NB,C)
        a=jnp.concatenate([v[0:F1,0:NB,:].reshape(M1,C),v[0:F1,NB:2*NB,:].reshape(M1,C),
            v[1:F1+1,0:NB,:].reshape(M1,C)],axis=1)
        g[0:M1,:]=jnp.dot(a,w1[...],preferred_element_type=F32)
    def el0(h,out,nxt):
        for r in range(0,M0,RG):
            v=act_rows(h[r:r+RG,:],EPS)
            out[E+r:E+r+RG,:]=v
            if r>=M0-E: nxt[r-(M0-E):r-(M0-E)+RG,:]=v
    def el1(i,g):
        for r in range(i*M1,(i+1)*M1,RG):
            act1[r:r+RG,:]=act_rows(g[r-i*M1:r-i*M1+RG,:],2*EPS)
    def step(i,par,m0=True,e0=True,m1=True,e1=True):
        if i+2<n: build_lhs(xf,lhs,(i+2)*2*F1,(i+3)*2*F1)
        if m0: mm0(i+1,hs[1-par])
        if m1: mm1(gs[1-par],pair[1-par])
        if e0: el0(hs[par],pair[par],pair[1-par])
        if e1: el1(i-2,gs[par])
    def edge(i):
        step(i,i%2,m0=i+1<n,e0=i<n,m1=0<=i-1<n,e1=0<=i-2<n)
    build_lhs(xf,lhs,0,4*F1)
    mm0(0,hs[0])
    for i in range(n+2): edge(i)

def extract(xf,w0,wm,wl,lhs,acts,hA,hB,gA,gB):
    first_two(xf,lhs,w0,wm.at[0],acts[0:2],acts[2],(hA,hB),(gA,gB))
    for l in range(2,7):
        T,Tc=PLAN[l]; M=Tc*NB; n=nchunk(l)
        out=acts[l+1]
        def mm(i,h,l=l,M=M,Tc=Tc):
            src=acts[l]
            s3=src.reshape(src.shape[0]//64,64,C)
            t0=i*Tc
            if l==2:
                a=[s3[pl.ds(t0,Tc),32:64,:],s3[pl.ds(t0+1,Tc),0:32,:],s3[pl.ds(t0+1,Tc),32:64,:]]
            else:
                a=[s3[pl.ds(t0,Tc),0:32,:],s3[pl.ds(t0,Tc),32:64,:]]
                if l<=4: a.append(s3[pl.ds(t0+1,Tc),0:32,:])
            a=[v.reshape(M,C) for v in a]
            w=wm[l-1] if l<=4 else wl[l-5]
            h[0:M,:]=jnp.dot(jnp.concatenate(a,axis=1),w,preferred_element_type=F32)
        def el(i,h,l=l,M=M,out=out):
            base=pl.multiple_of(i*M,M)
            def rows(r,_):
                out[pl.ds(base+r*RG,RG),:]=act_rows(h[pl.ds(r*RG,RG),:],2*EPS)
                return 0
            lax.fori_loop(0,M//RG,rows,0,unroll=True)
        pipeline(n,mm,el,hA,hB)

def act_scratch():
    frames=[2*F1+2,2*F1+2,138,68,34,16,8,4]
    return [pltpu.VMEM((f*NB,C),BF) for f in frames]
from jax.sharding import PartitionSpec as P


MESH=pl.DeviceIdType.MESH
I32=jnp.int32
ROWS=8
SHARDS=32
TILES=11
SLAB=48
SAMPLES=1360
WIDTH=1920
DEAD=2.0**100
def hops(k): return min(k//8,4-k//8)+min(k%8,8-k%8)
FAR_FIRST=sorted(range(1,SHARDS),key=lambda k:-hops(k))

def iota(shape,dim): return lax.broadcasted_iota(I32,shape,dim)
def earlier_counts(owned):
    tri=(iota((NB,NB),0)<iota((NB,NB),1)).astype(F32).astype(BF)
    return jnp.dot(owned.astype(F32).astype(BF),tri,preferred_element_type=F32)

def dp_peer(k):
    return lax.rem(lax.axis_index("dp")+k,ROWS)
def seq_peer(k):
    me=lax.axis_index("seq")
    return lax.rem(me//8+k//8,4)*8+lax.rem(lax.rem(me,8)+k%8,8)
def row_of_shard(s):
    return lax.rem(s,4)*8+s//4

def greet():
    barrier=pltpu.get_barrier_semaphore()
    def a(k,_):
        pl.semaphore_signal(barrier,inc=1,device_id={"dp":dp_peer(k)},device_id_type=MESH); return 0
    lax.fori_loop(1,ROWS,a,0)
    def b(k,_):
        pl.semaphore_signal(barrier,inc=1,device_id={"seq":seq_peer(k)},device_id_type=MESH); return 0
    lax.fori_loop(1,SHARDS,b,0)
    return barrier

def pack_waves(wave,packing,live,xa,tall,send):
    me=lax.axis_index("dp")
    xa[:,1280:1408]=jnp.zeros((NB,128),BF)
    xa[:,0:SAMPLES]=wave[...]
    table=packing[...]
    owned=(table>>5)==me
    count=earlier_counts(owned)
    parts=[]
    for i in range(4):
        chosen=owned&(count==float(i))
        index=jnp.sum(jnp.where(chosen,table&31,0),axis=1,keepdims=True)
        parts.append(jnp.where(iota((8,NB),1)==index,1.0,0.0))
    pick=jnp.concatenate(parts,axis=0)
    lives=jnp.sum(pick*live[...].astype(F32),axis=1,keepdims=True)
    pick=pick.astype(BF)
    y=jnp.dot(pick,xa[...],preferred_element_type=F32)
    for j in range(TILES):
        tile=y[:,j*128:(j+1)*128]
        if j==TILES-1:
            tile=jnp.where(iota((NB,128),1)==SAMPLES-1280,lives,tile)
        for i in range(4):
            tall[pl.ds(i*TILES+j,8,stride=SLAB),:]=tile[i*8:(i+1)*8,:]
    for d in range(ROWS):
        send[d]=tall[d*SLAB:(d+1)*SLAB,:].astype(BF)

def wave_copy(k,send,recv,ssem,rsem):
    return pltpu.make_async_remote_copy(src_ref=send.at[dp_peer(k)],dst_ref=recv.at[lax.axis_index("dp")],
        send_sem=ssem.at[k],recv_sem=rsem.at[k],device_id={"dp":dp_peer(k)},device_id_type=MESH)
def frame_copy(k,send,recv,ssem,rsem):
    return pltpu.make_async_remote_copy(src_ref=send.at[row_of_shard(seq_peer(k))],dst_ref=recv.at[lax.axis_index("seq")],
        send_sem=ssem.at[k],recv_sem=rsem.at[k],device_id={"seq":seq_peer(k)},device_id_type=MESH)

def order_rows(packing,placing):
    me_d,me_s=lax.axis_index("dp"),lax.axis_index("seq")
    own=packing[pl.ds(me_d,1),:]
    owned=(own>>5)==iota((ROWS,NB),0)
    count=earlier_counts(owned)
    slots=jnp.concatenate([jnp.where(owned&(count==float(i)),1.0,0.0) for i in range(4)],axis=0)
    table=placing[...]
    parts=[]
    for g in range(4):
        mine=((table>>5)==me_s)&((iota((8,128),1)>>5)==g)
        index=jnp.sum(jnp.where(mine,table&31,0),axis=1,keepdims=True)
        parts.append(jnp.where(iota((8,NB),1)==index,1.0,0.0))
    taken=jnp.concatenate(parts,axis=0)
    return lax.dot_general(taken.astype(BF),slots.astype(BF),(((1,),(1,)),((),())),preferred_element_type=F32).astype(BF)

def unpack_waves(recv,order,tall,xa,xf):
    for r in range(ROWS):
        tall[r*SLAB:(r+1)*SLAB,:]=recv[r].astype(F32)
    for j in range(TILES):
        tile=jnp.concatenate([tall[pl.ds(i*TILES+j,8,stride=SLAB),:] for i in range(4)],axis=0)
        xa[:,j*128:(j+1)*128]=tile.astype(BF)
    xf[:,0:1408]=jnp.dot(order,xa[...],preferred_element_type=F32)
    xf[:,1408:1536]=jnp.zeros((NB,128),F32)

def frame_order(placing):
    me=lax.axis_index("seq")
    row=placing[pl.ds(me//4,1),:]
    at=lax.rem(me,4)*32
    shape=(128,128)
    hit=iota(shape,1)==at+(iota(shape,0)>>2)
    source=jnp.sum(jnp.where(hit,row>>5,0),axis=1,keepdims=True)
    return jnp.where(iota(shape,1)==source*4+(iota(shape,0)&3),1.0,0.0).astype(BF)

def pack_frames(act,lives,gain,bias,tall,send):
    for f in range(4):
        a=act[f*NB:(f+1)*NB,:].astype(F32)
        d=a-jnp.mean(a,axis=1,keepdims=True)
        v=jnp.mean(d*d,axis=1,keepdims=True)
        ready=d*lax.rsqrt(v+2*EPS)*gain[...]+bias[...]
        ready=jnp.where(lives>f+0.5,ready,DEAD)
        for j in range(4):
            tall[pl.ds(f*4+j,NB,stride=16),:]=ready[:,j*128:(j+1)*128]
    for b in range(NB):
        send[b]=tall[b*16:(b+1)*16,:].astype(BF)

def unpack_frames(recv,order,tall,proj,proj_bias,out):
    for s in range(SHARDS):
        tall[s*16:(s+1)*16,:]=recv[s].astype(F32)
    a=jnp.concatenate([tall[pl.ds(j,128,stride=4),:] for j in range(4)],axis=1).astype(BF)
    ready=jnp.dot(order,a,preferred_element_type=F32)
    dead=ready[:,0:1]>DEAD/2
    ready=ready.astype(BF)
    for j in range(0,WIDTH,384):
        p=jnp.dot(ready,proj[:,j:j+384],preferred_element_type=F32)+proj_bias[:,j:j+384]
        out[:,j:j+384]=jnp.where(dead,0.0,p).astype(BF)

def center_all(ref,depth,copies):
    for l in range(ref.shape[0]):
        copies[l].wait()
        def b(i,_):
            r=pl.ds(pl.multiple_of(i*512,512),512)
            ref[l,r,:]=center(ref[l,r,:]).astype(BF); return 0
        lax.fori_loop(0,depth//512,b,0)

def mega(wave,packing,live,placing,w0,wm_h,wl_h,gain,bias,proj_h,proj_bias,out,
         xf,w0s,wm,wl,lhs,*rest):
    acts=rest[:8]
    hA,hB,gA,gB,proj,xa,tall,tall2,send1,recv1,send2,recv2,wsem,s1,r1,s2,r2=rest[8:]
    cps=[pltpu.make_async_copy(wm_h.at[l],wm.at[l],wsem.at[l]) for l in range(4)]
    cps+=[pltpu.make_async_copy(wl_h.at[l],wl.at[l],wsem.at[4+l]) for l in range(2)]
    cps+=[pltpu.make_async_copy(proj_h,proj,wsem.at[6])]
    for c in cps: c.start()
    barrier=greet()
    pack_waves(wave,packing,live,xa,tall,send1)
    pl.semaphore_wait(barrier,ROWS-1+SHARDS-1)
    def go(k,_):
        wave_copy(k,send1,recv1,s1,r1).start(); return 0
    lax.fori_loop(1,ROWS,go,0)
    me=lax.axis_index("dp")
    recv1[me]=send1[me]
    order=order_rows(packing,placing)
    forder=frame_order(placing)
    wc=center(w0[...]); hi=wc.astype(BF)
    w0s[...]=jnp.zeros((256,C),BF)
    w0s[0:10,:]=hi; w0s[128:138,:]=(wc-hi.astype(F32)).astype(BF)
    center_all(wm,1536,cps[0:4]); center_all(wl,1024,cps[4:6])
    def done(k,_):
        wave_copy(k,send1,recv1,s1,r1).wait(); return 0
    lax.fori_loop(1,ROWS,done,0)
    unpack_waves(recv1,order,tall,xa,xf)
    extract(xf,w0s,wm,wl,lhs,acts,hA,hB,gA,gB)
    lives=jnp.sum(jnp.where(iota((NB,128),1)==SAMPLES-1280,xf[:,1280:1408],0.0),axis=1,keepdims=True)
    pack_frames(acts[7],lives,gain,bias,tall2,send2)
    for k in FAR_FIRST: frame_copy(k,send2,recv2,s2,r2).start()
    ms=lax.axis_index("seq")
    recv2[ms]=send2[row_of_shard(ms)]
    def done2(k,_):
        frame_copy(k,send2,recv2,s2,r2).wait(); return 0
    lax.fori_loop(1,SHARDS,done2,0)
    cps[6].wait()
    unpack_frames(recv2,forder,tall2,proj,proj_bias,out)

def call_mega(wave,packing,live,placing,w0,wm,wl,g,b,proj,proj_bias):
    V=pl.BlockSpec(memory_space=pltpu.VMEM); A=pl.BlockSpec(memory_space=pl.ANY)
    D=pltpu.SemaphoreType.DMA
    return pl.pallas_call(mega,out_shape=pltpu.VMEM((128,WIDTH),BF),
     in_specs=[V,V,V,V,V,A,A,V,V,A,V],out_specs=V,
     scratch_shapes=[pltpu.VMEM((32,1536),F32),pltpu.VMEM((256,C),BF),pltpu.VMEM((4,1536,C),BF),pltpu.VMEM((2,1024,C),BF),
       pltpu.VMEM((272*32,128),BF)]+act_scratch()+[pltpu.VMEM((HM,C),F32)]*2+[pltpu.VMEM((GM,C),F32)]*2+[pltpu.VMEM((C,WIDTH),BF),
       pltpu.VMEM((NB,1408),BF),pltpu.VMEM((ROWS*SLAB,128),F32),pltpu.VMEM((SHARDS*16,128),F32),
       pltpu.VMEM((ROWS,SLAB,128),BF),pltpu.VMEM((ROWS,SLAB,128),BF),pltpu.VMEM((SHARDS,16,128),BF),pltpu.VMEM((SHARDS,16,128),BF),
       D((7,)),D((ROWS,)),D((ROWS,)),D((SHARDS,)),D((SHARDS,))],
     compiler_params=pltpu.CompilerParams(vmem_limit_bytes=60*2**20,collective_id=0,has_side_effects=True),name="extract")(
       wave,packing,live,placing,w0,wm,wl,g,b,proj,proj_bias)


def body(
    waveform,
    packing,
    live_frames,
    placing,
    first_kernel,
    middle_kernels,
    last_kernels,
    norm_gain,
    norm_bias,
    projection,
    projection_bias,
):
    encoded = call_mega(
        waveform[0],
        packing,
        live_frames,
        placing.reshape(8, 128),
        first_kernel,
        middle_kernels,
        last_kernels,
        norm_gain.reshape(1, C),
        norm_bias.reshape(1, C),
        projection,
        projection_bias.reshape(1, WIDTH),
    )
    return encoded[None]


def solution(mesh):
    placed = (
        P("dp", "seq", None),
        P(None, "seq"),
        P("dp", "seq"),
        P("dp", None),
        P(),
        P(),
        P(),
        P(),
        P(),
        P(),
        P(),
    )
    return jax.shard_map(
        body, mesh=mesh, in_specs=placed, out_specs=P("dp", "seq", None), check_vma=False
    )
```
